32 devices in a mesh: grp: 2 (over y), dp: 4 (over z), tensor: 4 (over x, core).
Axes of the slice: x: 2, y: 2, z: 4, core: 2. Of those that a mesh axis runs over, the one named last changes fastest.
Arguments:
- queries: bfloat16 [256, 8192], P(('grp', 'dp'), 'tensor'), parts along dimension 0, may hold values from -128 to 128
- key_value_cache: bfloat16 [256, 8, 2, 1024], P(('grp', 'dp'), None, None, 'tensor'), parts along dimension 0, may hold values from -7 to 7
- key_value_lengths: int32 [256], P(('grp', 'dp')), parts along dimension 0, may hold values from 1 to 8, as said below
- adapter_index: int32 [256], P(('grp', 'dp')), parts along dimension 0, may hold values from 0 to 3, as said below
- adapter_down_weight: bfloat16 [4, 64, 8192], P('dp', None, 'tensor'), may hold values from -0.0625 to 0.0625
- adapter_up_weight: bfloat16 [4, 64, 8192], P(None, None, 'dp'), may hold values from -0.75 to 0.75
- output_weight: bfloat16 [8192, 8192], P('tensor', 'dp'), may hold values from -0.0625 to 0.0625
Outputs:
- mixed: bfloat16 [256, 8192], P(('grp', 'tensor'), 'dp'), parts along dimension 0
- moved_cache: bfloat16 [512, 8, 2, 1024], P(('grp', 'dp'), None, None, 'tensor'), parts along dimension 0
The draws below stay inside these ranges and needn't reach their ends.
There are 2 independent parts, one for each index of `grp`. The reference program is written for one: setup_inputs(seed, part) draws one part's arguments, and reference() takes and returns one part's arrays. A program takes and returns all parts, laid end to end along the dimension named above; an argument that names none is the same for every part. Nothing has to cross between parts.
Inputs may be any that keep to these rules, and one draw needn't show every extreme that they name: `adapter_index`: among the 32 requests of one home rank at most 16 name the same adapter. `key_value_lengths`: the largest is 8.
All inputs are finite; a program needn't handle non-finite values.
Results may differ from the reference program's by a relative error of at most 0.0065.
Values may be sent and summed in bfloat16 or wider, within the bound.
A program may use at most 64 MiB of HBM per device.

```python
import math
import jax
import jax.numpy as jnp
from jax import lax

MODEL_WIDTH = 8192
KVD = 1024
HD = 128
ADAPTER_RANK = 64
REQUESTS_PER_DP = 32
LEN = 8
CAP = 16
REQUESTS = 128
ADAPTER_COUNT = 4
N_DP = 4
N_TENSOR = 4


def cache_values(key):
    base = jax.random.normal(jax.random.fold_in(key, 11), (REQUESTS, LEN, 2, KVD), jnp.float32)
    base = jnp.clip(base, -6.0, 6.0)
    picked = jax.random.randint(jax.random.fold_in(key, 12), (REQUESTS,), 0, 8) == 0
    second = jnp.where(picked[:, None], base[:, 0, 0, :], base[:, 1, 0, :])
    return base.at[:, 1, 0, :].set(second)


def draw_queries(key, part):
    key = jax.random.fold_in(key, 5)
    result = jnp.clip(jax.random.normal(key, (REQUESTS, MODEL_WIDTH), jnp.float32), -6.0, 6.0)
    return result.astype(jnp.bfloat16)


def draw_key_value_cache(key, part):
    values = cache_values(key)
    return values.astype(jnp.bfloat16)


def draw_key_value_lengths(key, part):
    key = jax.random.fold_in(key, 3)
    lengths = jax.random.randint(key, (REQUESTS,), 1, LEN + 1)
    chosen = jax.random.randint(jax.random.fold_in(key, 4), (), 0, REQUESTS)
    return jnp.where(jnp.arange(REQUESTS) == chosen, LEN, lengths).astype(jnp.int32)


def draw_adapter_index(key, part):
    key = jax.random.fold_in(key, 7)
    slots = N_DP * CAP
    busiest = jax.random.randint(jax.random.fold_in(key, 1), (), 0, N_DP)

    def one_block(index):
        block_key = jax.random.fold_in(key, index + 100)
        order = jax.random.permutation(block_key, slots)
        score = jnp.where(jnp.arange(slots) // CAP == busiest, -1, order)
        picked = jnp.argsort(score, stable=True)[:REQUESTS_PER_DP]
        shuffle = jax.random.permutation(jax.random.fold_in(block_key, 2), REQUESTS_PER_DP)
        return (picked[shuffle] // CAP).astype(jnp.int32)
    return jax.vmap(one_block)(jnp.arange(N_DP)).reshape(REQUESTS).astype(jnp.int32)


def shard_levels(stream_key, extent, shards, smallest, top_value):
    def one(axis_at, blocks):
        heights = jax.random.uniform(jax.random.fold_in(jax.random.fold_in(stream_key, 6), axis_at), (blocks,), jnp.float32, smallest / len(shards), top_value / len(shards))
        return jnp.repeat(jnp.exp(heights), extent[axis_at] // blocks).reshape((-1,) + (1,) * (len(extent) - axis_at - 1))

    level = one(*shards[0])
    for cut in shards[1:]:
        level = level * one(*cut)
    return level


def bell_draw(stream_key, shape, deviation, limit, cuts=(), held_as=jnp.bfloat16):
    array = deviation * jax.random.normal(stream_key, shape, jnp.float32)
    if cuts:
        array = array * shard_levels(stream_key, shape, cuts, -0.22, 0.18)
    return jnp.clip(array, -limit, limit).astype(held_as)


def setup_inputs(seed: int = 0, part: int = 0) -> dict:
    key_of = jax.random.split(jax.random.key(seed), 8)
    part_splits = jax.random.split(jax.random.fold_in(key_of[7], part), 8)
    queries = draw_queries(jax.random.fold_in(jax.random.fold_in(key_of[7], part), 71), part)
    key_value_cache = draw_key_value_cache(jax.random.fold_in(jax.random.fold_in(key_of[7], part), 71), part)
    key_value_lengths = draw_key_value_lengths(jax.random.fold_in(jax.random.fold_in(key_of[7], part), 71), part)
    adapter_index = draw_adapter_index(jax.random.fold_in(jax.random.fold_in(key_of[7], part), 71), part)
    adapter_down_weight = bell_draw(key_of[4], (ADAPTER_COUNT, ADAPTER_RANK, MODEL_WIDTH), MODEL_WIDTH ** -0.5, 0.0625, ((0, 4), (2, 4)))
    adapter_up_weight = bell_draw(key_of[5], (ADAPTER_COUNT, ADAPTER_RANK, MODEL_WIDTH), ADAPTER_RANK ** -0.5, 0.75, ((2, 4),))
    output_weight = bell_draw(key_of[6], (MODEL_WIDTH, MODEL_WIDTH), MODEL_WIDTH ** -0.5, 0.0625, ((0, 4), (1, 4)))
    return dict(queries=queries, key_value_cache=key_value_cache, key_value_lengths=key_value_lengths, adapter_index=adapter_index, adapter_down_weight=adapter_down_weight, adapter_up_weight=adapter_up_weight, output_weight=output_weight)


def earlier_same(targets):
    count = targets.shape[0]
    order = jnp.arange(count, dtype=jnp.int32)
    same = targets[:, None] == targets[None, :]
    before = order[None, :] < order[:, None]
    return lax.optimization_barrier(jnp.sum(jnp.where(same & before, 1, 0), axis=1)).astype(jnp.int32)

def attend(queries, cache, lengths):
    count = queries.shape[0]
    width = cache.shape[-1]
    kv_heads = width // HD
    group = queries.shape[1] // width
    query = queries.astype(jnp.float32).reshape(count, kv_heads, group, HD)
    keys = cache[:, :, 0, :].astype(jnp.float32).reshape(count, -1, kv_heads, HD)
    values = cache[:, :, 1, :].astype(jnp.float32).reshape(count, -1, kv_heads, HD)
    scores = jnp.einsum('rhgd,rlhd->rhgl', query, keys, precision=lax.Precision.HIGHEST) * (1.0 / math.sqrt(HD))
    position = jnp.arange(keys.shape[1], dtype=jnp.int32)
    live = position[None, None, None, :] < lengths[:, None, None, None]
    scores = jnp.where(live, scores, -1e+30)
    highest = lax.optimization_barrier(jnp.max(scores, axis=-1, keepdims=True))
    powers = jnp.exp(scores - highest)
    weights = (powers / lax.optimization_barrier(jnp.sum(powers, axis=-1, keepdims=True))).astype(jnp.bfloat16)
    output = jnp.einsum('rhgl,rlhd->rhgd', weights.astype(jnp.float32), values, precision=lax.Precision.HIGHEST)
    return output.reshape(count, -1).astype(jnp.bfloat16)

def reference(queries, key_value_cache, key_value_lengths, adapter_index, adapter_down_weight, adapter_up_weight, output_weight):
    slots = N_DP * CAP
    request_block = MODEL_WIDTH // N_TENSOR

    def home_rank(index):
        start = (index * REQUESTS_PER_DP).astype(jnp.int32)
        query = lax.dynamic_slice_in_dim(queries, start, REQUESTS_PER_DP, 0)
        cache = lax.dynamic_slice_in_dim(key_value_cache, start, REQUESTS_PER_DP, 0)
        lengths = lax.dynamic_slice_in_dim(key_value_lengths, start, REQUESTS_PER_DP, 0)
        adapter_table = lax.dynamic_slice_in_dim(adapter_index, start, REQUESTS_PER_DP, 0)
        attended_rows = attend(query, cache, lengths)
        down_product = adapter_down_weight[adapter_table].astype(jnp.float32).reshape(REQUESTS_PER_DP, ADAPTER_RANK, N_TENSOR, request_block)
        pieces = attended_rows.astype(jnp.float32).reshape(REQUESTS_PER_DP, N_TENSOR, request_block)
        lowered = jnp.einsum('rtk,rjtk->rtj', pieces, down_product, precision=lax.Precision.HIGHEST).astype(jnp.bfloat16)
        low_total = lax.optimization_barrier(jnp.sum(lowered.astype(jnp.float32), axis=1))
        up_product = adapter_up_weight[adapter_table].astype(jnp.float32)
        delta = jnp.einsum('rj,rjf->rf', low_total, up_product, precision=lax.Precision.HIGHEST)
        base = jnp.dot(attended_rows, output_weight, preferred_element_type=jnp.float32)
        result = (base + delta).astype(jnp.bfloat16)
        serve_row = adapter_table * slots + index.astype(jnp.int32) * CAP + earlier_same(adapter_table)
        return (result, serve_row.astype(jnp.int32))
    results, serve_rows = lax.map(home_rank, jnp.arange(N_DP, dtype=jnp.int32))
    mixed = results.reshape(REQUESTS, MODEL_WIDTH)
    moved_cache = jnp.zeros((N_DP * slots, LEN, 2, KVD), jnp.bfloat16).at[serve_rows.reshape(REQUESTS)].set(key_value_cache)
    return (mixed, moved_cache)
```

```python
import functools
import math

import jax
import jax.numpy as jnp
from jax import lax
from jax.experimental import pallas as pl
from jax.experimental.pallas import tpu as pltpu
from jax.sharding import PartitionSpec as P

HD = 128
LANES = 128
MESH = pl.DeviceIdType.MESH
F32 = jnp.float32
BF16 = jnp.bfloat16


def nt_dot(a, b):
    return lax.dot_general(a, b, (((1,), (1,)), ((), ())), preferred_element_type=F32)


def dot(a, b):
    return jnp.dot(a, b, preferred_element_type=F32)


def iota(shape, axis):
    return lax.broadcasted_iota(jnp.int32, shape, axis)


def flag(cond):
    return jnp.where(cond, 1.0, 0.0).astype(BF16)


def fused_kernel(
    peers,
    blocks,
    width,
    q_ref,
    cache_ref,
    len_ref,
    id_ref,
    down_hbm,
    up_hbm,
    w_hbm,
    mixed_ref,
    moved_ref,
    w_buf,
    up_buf,
    down_buf,
    att_buf,
    spread_buf,
    low_buf,
    base_buf,
    part_buf,
    part_recv,
    load_sem,
    att_send,
    att_recv,
    cache_send,
    cache_recv,
    low_send,
    low_recv,
    part_send_sem,
    part_recv_sem,
):
    dp = lax.axis_index("dp")
    tp = lax.axis_index("tensor")
    count, feats = q_ref.shape
    capacity = spread_buf.shape[1]
    out_width = w_buf.shape[1]
    chunks = part_recv.shape[0]
    chunk = out_width // chunks
    kv_heads = width // HD
    group = feats // width
    positions = cache_ref.shape[1] // (2 * width)

    loads = [
        pltpu.make_async_copy(down_hbm, down_buf, load_sem.at[0]),
        pltpu.make_async_copy(w_hbm, w_buf, load_sem.at[1]),
        pltpu.make_async_copy(up_hbm, up_buf, load_sem.at[2]),
    ]
    for load in loads:
        load.start()

    barrier = pltpu.get_barrier_semaphore()
    for d in range(1, peers):
        pl.semaphore_signal(
            barrier, inc=1, device_id={"dp": lax.rem(dp + d, peers)}, device_id_type=MESH
        )
    for d in range(1, blocks):
        pl.semaphore_signal(
            barrier, inc=1, device_id={"tensor": lax.rem(tp + d, blocks)}, device_id_type=MESH
        )

    rows, cols = group * count, positions * count
    row_request = iota((rows, cols), 0) & (count - 1)
    col_index = iota((rows, cols), 1)
    col_request = col_index & (count - 1)
    tile_requests = flag(
        iota((count, cols), 0) == (iota((count, cols), 1) & (count - 1))
    )
    lengths = jnp.broadcast_to(len_ref[...], (16, count)).astype(F32).astype(BF16)
    limit = dot(lengths, tile_requests)[0:1, :] * float(count)
    live = (row_request == col_request) & (col_index.astype(F32) < limit)
    for g in range(kv_heads):
        query = jnp.concatenate(
            [q_ref[:, (g * group + h) * HD : (g * group + h + 1) * HD] for h in range(group)], 0
        )
        keys = jnp.concatenate(
            [
                cache_ref[:, 2 * j * width + g * HD : 2 * j * width + (g + 1) * HD]
                for j in range(positions)
            ],
            0,
        )
        values = jnp.concatenate(
            [
                cache_ref[:, (2 * j + 1) * width + g * HD : (2 * j + 1) * width + (g + 1) * HD]
                for j in range(positions)
            ],
            0,
        )
        scores = jnp.where(live, nt_dot(query, keys) * (1.0 / math.sqrt(HD)), -1e30)
        powers = jnp.exp(scores - jnp.max(scores, axis=1, keepdims=True))
        weights = (powers / jnp.sum(powers, axis=1, keepdims=True)).astype(BF16)
        output = dot(weights, values).astype(BF16)
        for h in range(group):
            att_buf[dp, :, (g * group + h) * HD : (g * group + h + 1) * HD] = output[
                h * count : (h + 1) * count
            ]

    ids = jnp.broadcast_to(id_ref[...], (LANES, count))
    chosen = iota((LANES, count), 0) == ids
    chosen_flag = flag(chosen)
    eye = flag(iota((count, count), 0) == iota((count, count), 1))
    att_buf[dp, :, feats : feats + LANES] = nt_dot(eye, chosen_flag).astype(BF16)

    pl.semaphore_wait(barrier, peers - 1 + blocks - 1)
    att_copies = []
    for d in range(1, peers):
        copy = pltpu.make_async_remote_copy(
            src_ref=att_buf.at[dp],
            dst_ref=att_buf.at[dp],
            send_sem=att_send.at[d - 1],
            recv_sem=att_recv.at[d - 1],
            device_id={"dp": lax.rem(dp + d, peers)},
            device_id_type=MESH,
        )
        copy.start()
        att_copies.append(copy)

    earlier = flag(iota((count, count), 0) < iota((count, count), 1))
    before = dot(chosen_flag, earlier)
    rank = jnp.sum(jnp.where(chosen, before, 0.0), axis=0, keepdims=True)
    place = id_ref[...].astype(F32) * float(capacity) + rank
    slots = peers * capacity
    move = flag(iota((slots, count), 0).astype(F32) == place)
    step = 512
    for c in range(cache_ref.shape[1] // step):
        piece = dot(move, cache_ref[:, c * step : (c + 1) * step]).astype(BF16)
        spread_buf[:, :, c * step : (c + 1) * step] = piece.reshape(peers, capacity, step)
    cache_copies = []
    for d in range(1, peers):
        target = lax.rem(dp + d, peers)
        copy = pltpu.make_async_remote_copy(
            src_ref=spread_buf.at[target],
            dst_ref=moved_ref.at[dp],
            send_sem=cache_send.at[d - 1],
            recv_sem=cache_recv.at[d - 1],
            device_id={"dp": target},
            device_id_type=MESH,
        )
        copy.start()
        cache_copies.append(copy)
    own = pltpu.make_async_copy(spread_buf.at[dp], moved_ref.at[dp], load_sem.at[3])
    own.start()

    for copy in att_copies:
        copy.wait_recv()
    height = peers * count
    att = att_buf[:, :, :feats].reshape(height, feats)
    member = att_buf[:, :, feats : feats + LANES].reshape(height, LANES)
    loads[0].wait()
    low_rank = down_buf.shape[1]
    held = flag(iota((LANES, low_rank), 0) == dp)
    low = nt_dot(att, down_buf[0]) * dot(member, held)
    low_buf[dp] = low.astype(BF16)
    low_copies = []
    for d in range(1, peers):
        copy = pltpu.make_async_remote_copy(
            src_ref=low_buf.at[dp],
            dst_ref=low_buf.at[dp],
            send_sem=low_send.at[d - 1],
            recv_sem=low_recv.at[d - 1],
            device_id={"dp": lax.rem(dp + d, peers)},
            device_id_type=MESH,
        )
        copy.start()
        low_copies.append(copy)

    loads[1].wait()
    for c in range(chunks):
        base_buf[:, c * chunk : (c + 1) * chunk] = dot(att, w_buf[:, c * chunk : (c + 1) * chunk])
    loads[2].wait()
    for copy in low_copies:
        copy.wait_recv()

    expanded = jnp.concatenate([low_buf[a] for a in range(peers)], axis=1)
    part_copies = []
    for c in range(chunks):
        at = slice(c * chunk, (c + 1) * chunk)
        up = up_buf[:, :, at].reshape(peers * low_rank, chunk)
        total = base_buf[:, at] + dot(expanded, up)
        part_buf[c] = total.astype(BF16).reshape(blocks, height // blocks, chunk)
        for d in range(1, blocks):
            target = lax.rem(tp + d, blocks)
            copy = pltpu.make_async_remote_copy(
                src_ref=part_buf.at[c, target],
                dst_ref=part_recv.at[c, d - 1],
                send_sem=part_send_sem.at[c, d - 1],
                recv_sem=part_recv_sem.at[c, d - 1],
                device_id={"tensor": target},
                device_id_type=MESH,
            )
            copy.start()
            part_copies.append(copy)
    for c in range(chunks):
        total = part_buf[c, tp].astype(F32)
        for d in range(1, blocks):
            part_copies[c * (blocks - 1) + d - 1].wait_recv()
            total = total + part_recv[c, d - 1].astype(F32)
        mixed_ref[:, c * chunk : (c + 1) * chunk] = total.astype(BF16)

    own.wait()
    for copy in cache_copies:
        copy.wait_recv()
    for copy in att_copies + cache_copies + low_copies + part_copies:
        copy.wait_send()


def fused_shards(
    peers,
    blocks,
    queries,
    key_value_cache,
    key_value_lengths,
    adapter_index,
    adapter_down_weight,
    adapter_up_weight,
    output_weight,
):
    count, feats = queries.shape
    capacity = max(2, 2 * count // peers)
    row = math.prod(key_value_cache.shape[1:])
    out_width = output_weight.shape[1]
    low_rank = adapter_down_weight.shape[1]
    height = peers * count
    chunks = 4
    chunk = out_width // chunks
    vmem = pl.BlockSpec(memory_space=pltpu.VMEM)
    hbm = pl.BlockSpec(memory_space=pl.ANY)
    dma = pltpu.SemaphoreType.DMA
    mixed, moved = pl.pallas_call(
        functools.partial(fused_kernel, peers, blocks, key_value_cache.shape[-1]),
        out_shape=(
            jax.ShapeDtypeStruct((height // blocks, out_width), BF16),
            jax.ShapeDtypeStruct((peers, capacity, row), BF16),
        ),
        in_specs=[vmem, vmem, vmem, vmem, hbm, hbm, hbm],
        out_specs=(vmem, hbm),
        scratch_shapes=[
            pltpu.VMEM(output_weight.shape, BF16),
            pltpu.VMEM(adapter_up_weight.shape, BF16),
            pltpu.VMEM(adapter_down_weight.shape, BF16),
            pltpu.VMEM((peers, count, feats + LANES), BF16),
            pltpu.VMEM((peers, capacity, row), BF16),
            pltpu.VMEM((peers, height, low_rank), BF16),
            pltpu.VMEM((height, out_width), F32),
            pltpu.VMEM((chunks, blocks, height // blocks, chunk), BF16),
            pltpu.VMEM((chunks, blocks - 1, height // blocks, chunk), BF16),
            dma((4,)),
            dma((peers - 1,)),
            dma((peers - 1,)),
            dma((peers - 1,)),
            dma((peers - 1,)),
            dma((peers - 1,)),
            dma((peers - 1,)),
            dma((chunks, blocks - 1)),
            dma((chunks, blocks - 1)),
        ],
        compiler_params=pltpu.CompilerParams(
            collective_id=0, has_side_effects=True, vmem_limit_bytes=56 * 1024 * 1024
        ),
        name="fused",
    )(
        queries,
        key_value_cache.reshape(count, row),
        key_value_lengths.reshape(1, count),
        adapter_index.reshape(1, count),
        adapter_down_weight,
        adapter_up_weight,
        output_weight,
    )
    return mixed, moved.reshape((peers * capacity,) + key_value_cache.shape[1:])


def earlier_same(targets):
    count = targets.shape[0]
    order = jnp.arange(count, dtype=jnp.int32)
    same = targets[:, None] == targets[None, :]
    before = order[None, :] < order[:, None]
    return jnp.sum(jnp.where(same & before, 1, 0), axis=1).astype(jnp.int32)


def attend(queries, cache, lengths):
    count = queries.shape[0]
    width = cache.shape[-1]
    kv_heads = width // HD
    group = queries.shape[1] // width
    query = queries.reshape(count, kv_heads, group, HD)
    keys = cache[:, :, 0, :].reshape(count, -1, kv_heads, HD)
    values = cache[:, :, 1, :].reshape(count, -1, kv_heads, HD)
    scores = jnp.einsum("rhgd,rlhd->rhgl", query, keys, preferred_element_type=jnp.float32) * (
        1.0 / math.sqrt(HD)
    )
    position = jnp.arange(keys.shape[1], dtype=jnp.int32)
    live = position[None, None, None, :] < lengths[:, None, None, None]
    scores = jnp.where(live, scores, -1e30)
    highest = jnp.max(scores, axis=-1, keepdims=True)
    powers = jnp.exp(scores - highest)
    weights = (powers / jnp.sum(powers, axis=-1, keepdims=True)).astype(jnp.bfloat16)
    output = jnp.einsum("rhgl,rlhd->rhgd", weights, values, preferred_element_type=jnp.float32)
    return output.reshape(count, -1).astype(jnp.bfloat16)


def down_projection(attended_rows, adapter_down_weight):
    product = lax.dot_general(
        attended_rows,
        adapter_down_weight[0],
        (((1,), (1,)), ((), ())),
        preferred_element_type=jnp.float32,
    )
    return product.astype(jnp.bfloat16)


def shards(
    queries,
    key_value_cache,
    key_value_lengths,
    adapter_index,
    adapter_down_weight,
    adapter_up_weight,
    output_weight,
):
    peers = lax.axis_size("dp")
    count = queries.shape[0]
    capacity = max(2, 2 * count // peers)
    slots = peers * capacity
    places = adapter_index * capacity + earlier_same(adapter_index)

    def spread(values):
        return jnp.zeros((slots,) + values.shape[1:], values.dtype).at[places].set(values)

    attended_rows = attend(queries, key_value_cache, key_value_lengths)
    moved_attended, moved_cache = (
        lax.all_to_all(spread(attended_rows), "dp", split_axis=0, concat_axis=0, tiled=True),
        lax.all_to_all(spread(key_value_cache), "dp", split_axis=0, concat_axis=0, tiled=True),
    )
    low_rank_output = down_projection(moved_attended, adapter_down_weight)
    lowered = lax.all_to_all(low_rank_output, "dp", split_axis=0, concat_axis=0, tiled=True)[places]
    adapter_table = adapter_up_weight.shape[0]
    device_rank = adapter_up_weight.shape[1]
    flattened_up = adapter_up_weight.reshape(
        adapter_table * device_rank, adapter_up_weight.shape[2]
    )
    part_attended = lax.all_gather(attended_rows, "dp", axis=0, tiled=True)
    part_lowered = lax.all_gather(lowered, "dp", axis=0, tiled=True)
    part_ids = lax.all_gather(adapter_index, "dp", axis=0, tiled=True)
    height = part_attended.shape[0]
    chosen = part_ids[:, None] == jnp.arange(adapter_table, dtype=jnp.int32)[None, :]
    expanded = jnp.where(chosen[:, :, None], part_lowered[:, None, :], jnp.zeros((), jnp.bfloat16))
    expanded = expanded.reshape(height, adapter_table * device_rank)
    request_block = jnp.dot(part_attended, output_weight, preferred_element_type=jnp.float32)
    request_block = request_block + jnp.dot(
        expanded, flattened_up, preferred_element_type=jnp.float32
    )
    mixed = lax.psum_scatter(request_block, "tensor", scatter_dimension=0, tiled=True).astype(
        jnp.bfloat16
    )
    return (mixed, moved_cache)


def solution(mesh):
    peers, blocks = mesh.shape["dp"], mesh.shape["tensor"]
    body = functools.partial(fused_shards, peers, blocks) if peers <= 4 else shards
    in_specs = (
        P(("grp", "dp"), "tensor"),
        P(("grp", "dp"), None, None, "tensor"),
        P(("grp", "dp")),
        P(("grp", "dp")),
        P("dp", None, "tensor"),
        P(None, None, "dp"),
        P("tensor", "dp"),
    )
    out_specs = (P(("grp", "tensor"), "dp"), P(("grp", "dp"), None, None, "tensor"))
    return jax.shard_map(body, mesh=mesh, in_specs=in_specs, out_specs=out_specs, check_vma=False)
```

```python
import functools
import math

import jax
import jax.numpy as jnp
from jax import lax
from jax.experimental import pallas as pl
from jax.experimental.pallas import tpu as pltpu
from jax.sharding import PartitionSpec as P

HD = 128
LANES = 128
CACHE_STEP = 3
MESH = pl.DeviceIdType.MESH
F32 = jnp.float32
BF16 = jnp.bfloat16


def nt_dot(a, b):
    return lax.dot_general(a, b, (((1,), (1,)), ((), ())), preferred_element_type=F32)


def dot(a, b):
    return jnp.dot(a, b, preferred_element_type=F32)


def iota(shape, axis):
    return lax.broadcasted_iota(jnp.int32, shape, axis)


def flag(cond):
    return jnp.where(cond, 1.0, 0.0).astype(BF16)


def fused_kernel(
    peers,
    blocks,
    width,
    q_ref,
    cache_ref,
    len_ref,
    id_ref,
    down_hbm,
    up_hbm,
    w_hbm,
    mixed_ref,
    moved_ref,
    w_buf,
    up_buf,
    down_buf,
    att_buf,
    spread_buf,
    low_buf,
    low_in,
    own_buf,
    part_buf,
    part_recv,
    load_sem,
    att_send,
    att_recv,
    cache_send,
    cache_recv,
    low_send,
    low_recv,
    part_send_sem,
    part_recv_sem,
):
    dp = lax.axis_index("dp")
    tp = lax.axis_index("tensor")
    count, feats = q_ref.shape
    capacity = spread_buf.shape[1]
    out_width = w_buf.shape[1]
    chunk = part_buf.shape[3]
    chunks = out_width // chunk
    kv_heads = width // HD
    group = feats // width
    positions = cache_ref.shape[1] // (2 * width)

    loads = [
        pltpu.make_async_copy(down_hbm, down_buf, load_sem.at[0]),
        pltpu.make_async_copy(w_hbm, w_buf, load_sem.at[1]),
        pltpu.make_async_copy(up_hbm, up_buf, load_sem.at[2]),
    ]
    for load in loads:
        load.start()

    barrier = pltpu.get_barrier_semaphore()
    for d in range(peers):
        for e in range(blocks):
            if d or e:
                pl.semaphore_signal(
                    barrier,
                    inc=1,
                    device_id={"dp": lax.rem(dp + d, peers), "tensor": lax.rem(tp + e, blocks)},
                    device_id_type=MESH,
                )

    rows, cols = group * count, positions * count
    row_request = iota((rows, cols), 0) & (count - 1)
    col_index = iota((rows, cols), 1)
    col_request = col_index & (count - 1)
    tile_requests = flag(
        iota((count, cols), 0) == (iota((count, cols), 1) & (count - 1))
    )
    lengths = jnp.broadcast_to(len_ref[...], (16, count)).astype(F32).astype(BF16)
    limit = dot(lengths, tile_requests)[0:1, :] * float(count)
    live = (row_request == col_request) & (col_index.astype(F32) < limit)
    for g in range(kv_heads):
        query = jnp.concatenate(
            [q_ref[:, (g * group + h) * HD : (g * group + h + 1) * HD] for h in range(group)], 0
        )
        keys = jnp.concatenate(
            [
                cache_ref[:, 2 * j * width + g * HD : 2 * j * width + (g + 1) * HD]
                for j in range(positions)
            ],
            0,
        )
        values = jnp.concatenate(
            [
                cache_ref[:, (2 * j + 1) * width + g * HD : (2 * j + 1) * width + (g + 1) * HD]
                for j in range(positions)
            ],
            0,
        )
        scores = jnp.where(live, nt_dot(query, keys) * (1.0 / math.sqrt(HD)), -1e30)
        powers = jnp.exp(scores - jnp.max(scores, axis=1, keepdims=True))
        weights = (powers / jnp.sum(powers, axis=1, keepdims=True)).astype(BF16)
        output = dot(weights, values).astype(BF16)
        for h in range(group):
            att_buf[dp, :, (g * group + h) * HD : (g * group + h + 1) * HD] = output[
                h * count : (h + 1) * count
            ]

    ids = jnp.broadcast_to(id_ref[...], (LANES, count))
    chosen = iota((LANES, count), 0) == ids
    chosen_flag = flag(chosen)
    eye = flag(iota((count, count), 0) == iota((count, count), 1))
    att_buf[dp, :, feats : feats + LANES] = nt_dot(eye, chosen_flag).astype(BF16)

    pl.semaphore_wait(barrier, peers * blocks - 1)

    def att_copy(source, way):
        return pltpu.make_async_remote_copy(
            src_ref=att_buf.at[source],
            dst_ref=att_buf.at[source],
            send_sem=att_send.at[source, way],
            recv_sem=att_recv.at[source],
            device_id={"dp": lax.rem(dp + (1 if way else peers - 1), peers)},
            device_id_type=MESH,
        )

    def pass_on(source, act):
        @pl.when((source <= dp) & (dp < peers - 1))
        def _():
            act(att_copy(source, 1))

        @pl.when((source >= dp) & (dp > 0))
        def _():
            act(att_copy(source, 0))

    others = [lax.rem(dp + d, peers) for d in range(1, peers)]
    pass_on(dp, lambda copy: copy.start())

    earlier = flag(iota((count, count), 0) < iota((count, count), 1))
    before = dot(chosen_flag, earlier)
    rank = jnp.sum(jnp.where(chosen, before, 0.0), axis=0, keepdims=True)
    place = id_ref[...].astype(F32) * float(capacity) + rank
    slots = peers * capacity
    move = flag(iota((slots, count), 0).astype(F32) == place)
    step = 512
    for c in range(cache_ref.shape[1] // step):
        piece = dot(move, cache_ref[:, c * step : (c + 1) * step]).astype(BF16)
        spread_buf[:, :, c * step : (c + 1) * step] = piece.reshape(peers, capacity, step)

    def cache_copy(target, source):
        return pltpu.make_async_remote_copy(
            src_ref=spread_buf.at[target],
            dst_ref=moved_ref.at[source],
            send_sem=cache_send.at[target],
            recv_sem=cache_recv.at[source],
            device_id={"dp": target},
            device_id_type=MESH,
        )

    own = pltpu.make_async_copy(spread_buf.at[dp], moved_ref.at[dp], load_sem.at[3])
    own.start()

    def low_copy(block, target, holder, part):
        return pltpu.make_async_remote_copy(
            src_ref=low_buf.at[block],
            dst_ref=low_in.at[holder, part],
            send_sem=low_send.at[block, target],
            recv_sem=low_recv.at[holder, part],
            device_id={"dp": target, "tensor": block},
            device_id_type=MESH,
        )

    def part_copy(block, part, c):
        return pltpu.make_async_remote_copy(
            src_ref=part_buf.at[block, c],
            dst_ref=part_recv.at[part, c],
            send_sem=part_send_sem.at[block, c],
            recv_sem=part_recv_sem.at[part, c],
            device_id={"tensor": block},
            device_id_type=MESH,
        )

    low_rank = down_buf.shape[1]
    held = flag(iota((LANES, low_rank), 0) == dp)
    loads[0].wait()
    loads[1].wait()

    def nearest(step):
        up = jnp.where(step - 1 < dp, step - 1, step)
        last = peers - step
        down = jnp.where(last > dp, last, last - 1)
        return jnp.where(step == 0, dp, jnp.where(dp < peers // 2, up, down))

    def arrive(step):
        source = nearest(step)
        att_copy(source, 0).wait_recv()
        pass_on(source, lambda copy: copy.start())

    inner = (dp > 0) & (dp < peers - 1)

    def work(step, carry):
        source = nearest(step)

        @pl.when((step > 0) & jnp.logical_not(inner & (step == 2)))
        def _():
            arrive(step)

        @pl.when((step == 1) & inner)
        def _():
            arrive(2)

        rows = att_buf[source, :, :feats]
        member = dot(att_buf[source, :, feats : feats + LANES], held)
        low_buf[source] = (nt_dot(rows, down_buf[0]) * member).astype(BF16)
        for target in others:
            low_copy(source, target, dp, tp).start()

        @pl.when(source != tp)
        def _():
            low_copy(source, dp, dp, tp).start()

        @pl.when(source == tp)
        def _():
            low_in[dp, tp] = low_buf[source]

        @pl.when(step == CACHE_STEP)
        def _():
            for target in others:
                cache_copy(target, dp).start()

        for c in range(chunks):
            at = slice(c * chunk, (c + 1) * chunk)
            part = dot(rows, w_buf[:, at])
            part_buf[source, c] = part.astype(BF16)

            @pl.when(source == tp)
            def _():
                own_buf[:, at] = part

            @pl.when(source != tp)
            def _():
                part_copy(source, tp, c).start()

        return carry

    lax.fori_loop(0, peers, work, 0)

    loads[2].wait()
    for d in range(peers):
        for e in range(blocks):
            if d or e:
                low_copy(tp, dp, lax.rem(dp + d, peers), lax.rem(tp + e, blocks)).wait_recv()
    lows = []
    for a in range(peers):
        total = low_in[a, 0].astype(F32)
        for t in range(1, blocks):
            total = total + low_in[a, t].astype(F32)
        lows.append(total)
    low_total = jnp.concatenate(lows, axis=1)
    high = low_total.astype(BF16)
    rest = (low_total - high.astype(F32)).astype(BF16)
    both = jnp.concatenate([high, rest], axis=0)
    for c in range(chunks):
        at = slice(c * chunk, (c + 1) * chunk)
        delta = dot(both, up_buf[:, :, at].reshape(peers * low_rank, chunk))
        own_buf[:, at] += delta[:count] + delta[count:]
    parts = [lax.rem(tp + e, blocks) for e in range(1, blocks)]
    for c in range(chunks):
        at = slice(c * chunk, (c + 1) * chunk)
        total = own_buf[:, at]
        for part in parts:
            part_copy(tp, part, c).wait_recv()
            total = total + part_recv[part, c].astype(F32)
        mixed_ref[:, at] = total.astype(BF16)

    own.wait()
    for source in others:
        cache_copy(dp, source).wait_recv()
    for target in others:
        cache_copy(target, dp).wait_send()
    for block in parts:
        for c in range(chunks):
            part_copy(block, tp, c).wait_send()
        low_copy(block, dp, dp, tp).wait_send()
    for block in range(blocks):
        pass_on(block, lambda copy: copy.wait_send())
        for target in others:
            low_copy(block, target, dp, tp).wait_send()


def fused_shards(
    peers,
    blocks,
    queries,
    key_value_cache,
    key_value_lengths,
    adapter_index,
    adapter_down_weight,
    adapter_up_weight,
    output_weight,
):
    count, feats = queries.shape
    capacity = max(2, 2 * count // peers)
    row = math.prod(key_value_cache.shape[1:])
    out_width = output_weight.shape[1]
    low_rank = adapter_down_weight.shape[1]
    height = peers * count
    chunks = 2
    vmem = pl.BlockSpec(memory_space=pltpu.VMEM)
    hbm = pl.BlockSpec(memory_space=pl.ANY)
    dma = pltpu.SemaphoreType.DMA
    mixed, moved = pl.pallas_call(
        functools.partial(fused_kernel, peers, blocks, key_value_cache.shape[-1]),
        out_shape=(
            jax.ShapeDtypeStruct((height // blocks, out_width), BF16),
            jax.ShapeDtypeStruct((peers, capacity, row), BF16),
        ),
        in_specs=[vmem, vmem, vmem, vmem, hbm, hbm, hbm],
        out_specs=(vmem, hbm),
        scratch_shapes=[
            pltpu.VMEM(output_weight.shape, BF16),
            pltpu.VMEM(adapter_up_weight.shape, BF16),
            pltpu.VMEM(adapter_down_weight.shape, BF16),
            pltpu.VMEM((peers, count, feats + LANES), BF16),
            pltpu.VMEM((peers, capacity, row), BF16),
            pltpu.VMEM((blocks, count, low_rank), BF16),
            pltpu.VMEM((peers, blocks, count, low_rank), BF16),
            pltpu.VMEM((count, out_width), F32),
            pltpu.VMEM((blocks, chunks, count, out_width // chunks), BF16),
            pltpu.VMEM((blocks, chunks, count, out_width // chunks), BF16),
            dma((4,)),
            dma((peers, 2)),
            dma((peers,)),
            dma((peers,)),
            dma((peers,)),
            dma((blocks, peers)),
            dma((peers, blocks)),
            dma((blocks, chunks)),
            dma((blocks, chunks)),
        ],
        compiler_params=pltpu.CompilerParams(
            collective_id=0, has_side_effects=True, vmem_limit_bytes=56 * 1024 * 1024
        ),
        name="fused",
    )(
        queries,
        key_value_cache.reshape(count, row),
        key_value_lengths.reshape(1, count),
        adapter_index.reshape(1, count),
        adapter_down_weight,
        adapter_up_weight,
        output_weight,
    )
    return mixed, moved.reshape((peers * capacity,) + key_value_cache.shape[1:])


def earlier_same(targets):
    count = targets.shape[0]
    order = jnp.arange(count, dtype=jnp.int32)
    same = targets[:, None] == targets[None, :]
    before = order[None, :] < order[:, None]
    return jnp.sum(jnp.where(same & before, 1, 0), axis=1).astype(jnp.int32)


def attend(queries, cache, lengths):
    count = queries.shape[0]
    width = cache.shape[-1]
    kv_heads = width // HD
    group = queries.shape[1] // width
    query = queries.reshape(count, kv_heads, group, HD)
    keys = cache[:, :, 0, :].reshape(count, -1, kv_heads, HD)
    values = cache[:, :, 1, :].reshape(count, -1, kv_heads, HD)
    scores = jnp.einsum("rhgd,rlhd->rhgl", query, keys, preferred_element_type=jnp.float32) * (
        1.0 / math.sqrt(HD)
    )
    position = jnp.arange(keys.shape[1], dtype=jnp.int32)
    live = position[None, None, None, :] < lengths[:, None, None, None]
    scores = jnp.where(live, scores, -1e30)
    highest = jnp.max(scores, axis=-1, keepdims=True)
    powers = jnp.exp(scores - highest)
    weights = (powers / jnp.sum(powers, axis=-1, keepdims=True)).astype(jnp.bfloat16)
    output = jnp.einsum("rhgl,rlhd->rhgd", weights, values, preferred_element_type=jnp.float32)
    return output.reshape(count, -1).astype(jnp.bfloat16)


def down_projection(attended_rows, adapter_down_weight):
    product = lax.dot_general(
        attended_rows,
        adapter_down_weight[0],
        (((1,), (1,)), ((), ())),
        preferred_element_type=jnp.float32,
    )
    return product.astype(jnp.bfloat16)


def shards(
    queries,
    key_value_cache,
    key_value_lengths,
    adapter_index,
    adapter_down_weight,
    adapter_up_weight,
    output_weight,
):
    peers = lax.axis_size("dp")
    count = queries.shape[0]
    capacity = max(2, 2 * count // peers)
    slots = peers * capacity
    places = adapter_index * capacity + earlier_same(adapter_index)

    def spread(values):
        return jnp.zeros((slots,) + values.shape[1:], values.dtype).at[places].set(values)

    attended_rows = attend(queries, key_value_cache, key_value_lengths)
    moved_attended, moved_cache = (
        lax.all_to_all(spread(attended_rows), "dp", split_axis=0, concat_axis=0, tiled=True),
        lax.all_to_all(spread(key_value_cache), "dp", split_axis=0, concat_axis=0, tiled=True),
    )
    low_rank_output = down_projection(moved_attended, adapter_down_weight)
    lowered = lax.all_to_all(low_rank_output, "dp", split_axis=0, concat_axis=0, tiled=True)[places]
    adapter_table = adapter_up_weight.shape[0]
    device_rank = adapter_up_weight.shape[1]
    flattened_up = adapter_up_weight.reshape(
        adapter_table * device_rank, adapter_up_weight.shape[2]
    )
    part_attended = lax.all_gather(attended_rows, "dp", axis=0, tiled=True)
    part_lowered = lax.all_gather(lowered, "dp", axis=0, tiled=True)
    part_ids = lax.all_gather(adapter_index, "dp", axis=0, tiled=True)
    height = part_attended.shape[0]
    chosen = part_ids[:, None] == jnp.arange(adapter_table, dtype=jnp.int32)[None, :]
    expanded = jnp.where(chosen[:, :, None], part_lowered[:, None, :], jnp.zeros((), jnp.bfloat16))
    expanded = expanded.reshape(height, adapter_table * device_rank)
    request_block = jnp.dot(part_attended, output_weight, preferred_element_type=jnp.float32)
    request_block = request_block + jnp.dot(
        expanded, flattened_up, preferred_element_type=jnp.float32
    )
    mixed = lax.psum_scatter(request_block, "tensor", scatter_dimension=0, tiled=True).astype(
        jnp.bfloat16
    )
    return (mixed, moved_cache)


def solution(mesh):
    peers, blocks = mesh.shape["dp"], mesh.shape["tensor"]
    body = functools.partial(fused_shards, peers, blocks) if peers == blocks <= 4 else shards
    in_specs = (
        P(("grp", "dp"), "tensor"),
        P(("grp", "dp"), None, None, "tensor"),
        P(("grp", "dp")),
        P(("grp", "dp")),
        P("dp", None, "tensor"),
        P(None, None, "dp"),
        P("tensor", "dp"),
    )
    out_specs = (P(("grp", "tensor"), "dp"), P(("grp", "dp"), None, None, "tensor"))
    return jax.shard_map(body, mesh=mesh, in_specs=in_specs, out_specs=out_specs, check_vma=False)
```

```python
import functools
import math

import jax
import jax.numpy as jnp
from jax import lax
from jax.experimental import pallas as pl
from jax.experimental.pallas import tpu as pltpu
from jax.sharding import PartitionSpec as P

HD = 128
LANES = 128
CACHE_STEP = 3
MESH = pl.DeviceIdType.MESH
F32 = jnp.float32
BF16 = jnp.bfloat16


def nt_dot(a, b):
    return lax.dot_general(a, b, (((1,), (1,)), ((), ())), preferred_element_type=F32)


def dot(a, b):
    return jnp.dot(a, b, preferred_element_type=F32)


def iota(shape, axis):
    return lax.broadcasted_iota(jnp.int32, shape, axis)


def flag(cond):
    return jnp.where(cond, 1.0, 0.0).astype(BF16)


def fused_kernel(
    peers,
    blocks,
    width,
    q_ref,
    cache_ref,
    len_ref,
    id_ref,
    down_hbm,
    up_hbm,
    w_hbm,
    mixed_ref,
    moved_ref,
    w_buf,
    up_buf,
    down_buf,
    att_buf,
    spread_buf,
    low_buf,
    low_in,
    own_buf,
    part_buf,
    part_recv,
    load_sem,
    att_send,
    att_recv,
    cache_send,
    cache_recv,
    low_send,
    low_recv,
    part_send_sem,
    part_recv_sem,
):
    dp = lax.axis_index("dp")
    tp = lax.axis_index("tensor")
    count, feats = q_ref.shape
    capacity = spread_buf.shape[1]
    out_width = w_buf.shape[1]
    chunk = part_buf.shape[3]
    chunks = out_width // chunk
    kv_heads = width // HD
    group = feats // width
    positions = cache_ref.shape[1] // (2 * width)

    loads = [
        pltpu.make_async_copy(down_hbm, down_buf, load_sem.at[0]),
        pltpu.make_async_copy(w_hbm, w_buf, load_sem.at[1]),
        pltpu.make_async_copy(up_hbm, up_buf, load_sem.at[2]),
    ]
    for load in loads:
        load.start()

    barrier = pltpu.get_barrier_semaphore()
    for d in range(peers):
        for e in range(blocks):
            if d or e:
                pl.semaphore_signal(
                    barrier,
                    inc=1,
                    device_id={"dp": lax.rem(dp + d, peers), "tensor": lax.rem(tp + e, blocks)},
                    device_id_type=MESH,
                )

    rows, cols = group * count, positions * count
    row_request = iota((rows, cols), 0) & (count - 1)
    col_index = iota((rows, cols), 1)
    col_request = col_index & (count - 1)
    tile_requests = flag(
        iota((count, cols), 0) == (iota((count, cols), 1) & (count - 1))
    )
    lengths = jnp.broadcast_to(len_ref[...], (16, count)).astype(F32).astype(BF16)
    limit = dot(lengths, tile_requests)[0:1, :] * float(count)
    live = (row_request == col_request) & (col_index.astype(F32) < limit)
    for g in range(kv_heads):
        query = jnp.concatenate(
            [q_ref[:, (g * group + h) * HD : (g * group + h + 1) * HD] for h in range(group)], 0
        )
        keys = jnp.concatenate(
            [
                cache_ref[:, 2 * j * width + g * HD : 2 * j * width + (g + 1) * HD]
                for j in range(positions)
            ],
            0,
        )
        values = jnp.concatenate(
            [
                cache_ref[:, (2 * j + 1) * width + g * HD : (2 * j + 1) * width + (g + 1) * HD]
                for j in range(positions)
            ],
            0,
        )
        scores = jnp.where(live, nt_dot(query, keys) * (1.0 / math.sqrt(HD)), -1e30)
        powers = jnp.exp(scores - jnp.max(scores, axis=1, keepdims=True))
        weights = (powers / jnp.sum(powers, axis=1, keepdims=True)).astype(BF16)
        output = dot(weights, values).astype(BF16)
        for h in range(group):
            att_buf[dp, :, (g * group + h) * HD : (g * group + h + 1) * HD] = output[
                h * count : (h + 1) * count
            ]

    ids = jnp.broadcast_to(id_ref[...], (LANES, count))
    chosen = iota((LANES, count), 0) == ids
    chosen_flag = flag(chosen)
    eye = flag(iota((count, count), 0) == iota((count, count), 1))
    att_buf[dp, :, feats : feats + LANES] = nt_dot(eye, chosen_flag).astype(BF16)

    pl.semaphore_wait(barrier, peers * blocks - 1)

    def att_copy(source, way):
        return pltpu.make_async_remote_copy(
            src_ref=att_buf.at[source],
            dst_ref=att_buf.at[source],
            send_sem=att_send.at[source, way],
            recv_sem=att_recv.at[source],
            device_id={"dp": lax.rem(dp + (1 if way else peers - 1), peers)},
            device_id_type=MESH,
        )

    def pass_on(source, act):
        @pl.when((source <= dp) & (dp < peers - 1))
        def _():
            act(att_copy(source, 1))

        @pl.when((source >= dp) & (dp > 0))
        def _():
            act(att_copy(source, 0))

    others = [lax.rem(dp + d, peers) for d in range(1, peers)]
    pass_on(dp, lambda copy: copy.start())

    earlier = flag(iota((count, count), 0) < iota((count, count), 1))
    before = dot(chosen_flag, earlier)
    rank = jnp.sum(jnp.where(chosen, before, 0.0), axis=0, keepdims=True)
    place = id_ref[...].astype(F32) * float(capacity) + rank
    slots = peers * capacity
    move = flag(iota((slots, count), 0).astype(F32) == place)
    step = 512
    for c in range(cache_ref.shape[1] // step):
        piece = dot(move, cache_ref[:, c * step : (c + 1) * step]).astype(BF16)
        spread_buf[:, :, c * step : (c + 1) * step] = piece.reshape(peers, capacity, step)

    def cache_copy(target, source):
        return pltpu.make_async_remote_copy(
            src_ref=spread_buf.at[target],
            dst_ref=moved_ref.at[source],
            send_sem=cache_send.at[target],
            recv_sem=cache_recv.at[source],
            device_id={"dp": target},
            device_id_type=MESH,
        )

    own = pltpu.make_async_copy(spread_buf.at[dp], moved_ref.at[dp], load_sem.at[3])
    own.start()

    def low_copy(block, target, holder, part):
        return pltpu.make_async_remote_copy(
            src_ref=low_buf.at[block],
            dst_ref=low_in.at[holder, part],
            send_sem=low_send.at[block, target],
            recv_sem=low_recv.at[holder, part],
            device_id={"dp": target, "tensor": block},
            device_id_type=MESH,
        )

    def part_copy(block, part, c):
        return pltpu.make_async_remote_copy(
            src_ref=part_buf.at[block, c],
            dst_ref=part_recv.at[part, c],
            send_sem=part_send_sem.at[block, c],
            recv_sem=part_recv_sem.at[part, c],
            device_id={"tensor": block},
            device_id_type=MESH,
        )

    low_rank = down_buf.shape[1]
    held = flag(iota((LANES, low_rank), 0) == dp)
    loads[0].wait()
    loads[1].wait()

    def nearest(step):
        up = jnp.where(step - 1 < dp, step - 1, step)
        last = peers - step
        down = jnp.where(last > dp, last, last - 1)
        return jnp.where(step == 0, dp, jnp.where(dp < peers // 2, up, down))

    def arrive(step):
        source = nearest(step)
        att_copy(source, 0).wait_recv()
        pass_on(source, lambda copy: copy.start())

    inward = jnp.where(dp < peers // 2, lax.rem(dp + 1, peers), jnp.maximum(dp - 1, 0))
    inner = (dp > 0) & (dp < peers - 1)

    def work(step, carry):
        source = nearest(step)

        @pl.when((step > 0) & jnp.logical_not(inner & (step == 2)))
        def _():
            arrive(step)

        @pl.when((step == 1) & inner)
        def _():
            arrive(2)

        @pl.when(step == CACHE_STEP - 1)
        def _():
            cache_copy(inward, dp).start()

        @pl.when(step == CACHE_STEP)
        def _():
            for target in others:

                @pl.when(target != inward)
                def _():
                    cache_copy(target, dp).start()

        rows = att_buf[source, :, :feats]
        member = dot(att_buf[source, :, feats : feats + LANES], held)
        low_buf[source] = (nt_dot(rows, down_buf[0]) * member).astype(BF16)
        for target in others:
            low_copy(source, target, dp, tp).start()

        @pl.when(source != tp)
        def _():
            low_copy(source, dp, dp, tp).start()

        @pl.when(source == tp)
        def _():
            low_in[dp, tp] = low_buf[source]

        for c in range(chunks):
            at = slice(c * chunk, (c + 1) * chunk)
            part = dot(rows, w_buf[:, at])
            part_buf[source, c] = part.astype(BF16)

            @pl.when(source == tp)
            def _():
                own_buf[:, at] = part

            @pl.when(source != tp)
            def _():
                part_copy(source, tp, c).start()

        return carry

    lax.fori_loop(0, peers, work, 0)

    loads[2].wait()
    for d in range(peers):
        for e in range(blocks):
            if d or e:
                low_copy(tp, dp, lax.rem(dp + d, peers), lax.rem(tp + e, blocks)).wait_recv()
    lows = []
    for a in range(peers):
        total = low_in[a, 0].astype(F32)
        for t in range(1, blocks):
            total = total + low_in[a, t].astype(F32)
        lows.append(total)
    low_total = jnp.concatenate(lows, axis=1)
    high = low_total.astype(BF16)
    rest = (low_total - high.astype(F32)).astype(BF16)
    both = jnp.concatenate([high, rest], axis=0)
    for c in range(chunks):
        at = slice(c * chunk, (c + 1) * chunk)
        delta = dot(both, up_buf[:, :, at].reshape(peers * low_rank, chunk))
        own_buf[:, at] += delta[:count] + delta[count:]
    parts = [lax.rem(tp + e, blocks) for e in range(1, blocks)]
    for c in range(chunks):
        at = slice(c * chunk, (c + 1) * chunk)
        total = own_buf[:, at]
        for part in parts:
            part_copy(tp, part, c).wait_recv()
            total = total + part_recv[part, c].astype(F32)
        mixed_ref[:, at] = total.astype(BF16)

    own.wait()
    for source in others:
        cache_copy(dp, source).wait_recv()
    for target in others:
        cache_copy(target, dp).wait_send()
    for block in parts:
        for c in range(chunks):
            part_copy(block, tp, c).wait_send()
        low_copy(block, dp, dp, tp).wait_send()
    for block in range(blocks):
        pass_on(block, lambda copy: copy.wait_send())
        for target in others:
            low_copy(block, target, dp, tp).wait_send()


def fused_shards(
    peers,
    blocks,
    queries,
    key_value_cache,
    key_value_lengths,
    adapter_index,
    adapter_down_weight,
    adapter_up_weight,
    output_weight,
):
    count, feats = queries.shape
    capacity = max(2, 2 * count // peers)
    row = math.prod(key_value_cache.shape[1:])
    out_width = output_weight.shape[1]
    low_rank = adapter_down_weight.shape[1]
    height = peers * count
    chunks = 2
    vmem = pl.BlockSpec(memory_space=pltpu.VMEM)
    hbm = pl.BlockSpec(memory_space=pl.ANY)
    dma = pltpu.SemaphoreType.DMA
    mixed, moved = pl.pallas_call(
        functools.partial(fused_kernel, peers, blocks, key_value_cache.shape[-1]),
        out_shape=(
            jax.ShapeDtypeStruct((height // blocks, out_width), BF16),
            jax.ShapeDtypeStruct((peers, capacity, row), BF16),
        ),
        in_specs=[vmem, vmem, vmem, vmem, hbm, hbm, hbm],
        out_specs=(vmem, hbm),
        scratch_shapes=[
            pltpu.VMEM(output_weight.shape, BF16),
            pltpu.VMEM(adapter_up_weight.shape, BF16),
            pltpu.VMEM(adapter_down_weight.shape, BF16),
            pltpu.VMEM((peers, count, feats + LANES), BF16),
            pltpu.VMEM((peers, capacity, row), BF16),
            pltpu.VMEM((blocks, count, low_rank), BF16),
            pltpu.VMEM((peers, blocks, count, low_rank), BF16),
            pltpu.VMEM((count, out_width), F32),
            pltpu.VMEM((blocks, chunks, count, out_width // chunks), BF16),
            pltpu.VMEM((blocks, chunks, count, out_width // chunks), BF16),
            dma((4,)),
            dma((peers, 2)),
            dma((peers,)),
            dma((peers,)),
            dma((peers,)),
            dma((blocks, peers)),
            dma((peers, blocks)),
            dma((blocks, chunks)),
            dma((blocks, chunks)),
        ],
        compiler_params=pltpu.CompilerParams(
            collective_id=0, has_side_effects=True, vmem_limit_bytes=56 * 1024 * 1024
        ),
        name="fused",
    )(
        queries,
        key_value_cache.reshape(count, row),
        key_value_lengths.reshape(1, count),
        adapter_index.reshape(1, count),
        adapter_down_weight,
        adapter_up_weight,
        output_weight,
    )
    return mixed, moved.reshape((peers * capacity,) + key_value_cache.shape[1:])


def earlier_same(targets):
    count = targets.shape[0]
    order = jnp.arange(count, dtype=jnp.int32)
    same = targets[:, None] == targets[None, :]
    before = order[None, :] < order[:, None]
    return jnp.sum(jnp.where(same & before, 1, 0), axis=1).astype(jnp.int32)


def attend(queries, cache, lengths):
    count = queries.shape[0]
    width = cache.shape[-1]
    kv_heads = width // HD
    group = queries.shape[1] // width
    query = queries.reshape(count, kv_heads, group, HD)
    keys = cache[:, :, 0, :].reshape(count, -1, kv_heads, HD)
    values = cache[:, :, 1, :].reshape(count, -1, kv_heads, HD)
    scores = jnp.einsum("rhgd,rlhd->rhgl", query, keys, preferred_element_type=jnp.float32) * (
        1.0 / math.sqrt(HD)
    )
    position = jnp.arange(keys.shape[1], dtype=jnp.int32)
    live = position[None, None, None, :] < lengths[:, None, None, None]
    scores = jnp.where(live, scores, -1e30)
    highest = jnp.max(scores, axis=-1, keepdims=True)
    powers = jnp.exp(scores - highest)
    weights = (powers / jnp.sum(powers, axis=-1, keepdims=True)).astype(jnp.bfloat16)
    output = jnp.einsum("rhgl,rlhd->rhgd", weights, values, preferred_element_type=jnp.float32)
    return output.reshape(count, -1).astype(jnp.bfloat16)


def down_projection(attended_rows, adapter_down_weight):
    product = lax.dot_general(
        attended_rows,
        adapter_down_weight[0],
        (((1,), (1,)), ((), ())),
        preferred_element_type=jnp.float32,
    )
    return product.astype(jnp.bfloat16)


def shards(
    queries,
    key_value_cache,
    key_value_lengths,
    adapter_index,
    adapter_down_weight,
    adapter_up_weight,
    output_weight,
):
    peers = lax.axis_size("dp")
    count = queries.shape[0]
    capacity = max(2, 2 * count // peers)
    slots = peers * capacity
    places = adapter_index * capacity + earlier_same(adapter_index)

    def spread(values):
        return jnp.zeros((slots,) + values.shape[1:], values.dtype).at[places].set(values)

    attended_rows = attend(queries, key_value_cache, key_value_lengths)
    moved_attended, moved_cache = (
        lax.all_to_all(spread(attended_rows), "dp", split_axis=0, concat_axis=0, tiled=True),
        lax.all_to_all(spread(key_value_cache), "dp", split_axis=0, concat_axis=0, tiled=True),
    )
    low_rank_output = down_projection(moved_attended, adapter_down_weight)
    lowered = lax.all_to_all(low_rank_output, "dp", split_axis=0, concat_axis=0, tiled=True)[places]
    adapter_table = adapter_up_weight.shape[0]
    device_rank = adapter_up_weight.shape[1]
    flattened_up = adapter_up_weight.reshape(
        adapter_table * device_rank, adapter_up_weight.shape[2]
    )
    part_attended = lax.all_gather(attended_rows, "dp", axis=0, tiled=True)
    part_lowered = lax.all_gather(lowered, "dp", axis=0, tiled=True)
    part_ids = lax.all_gather(adapter_index, "dp", axis=0, tiled=True)
    height = part_attended.shape[0]
    chosen = part_ids[:, None] == jnp.arange(adapter_table, dtype=jnp.int32)[None, :]
    expanded = jnp.where(chosen[:, :, None], part_lowered[:, None, :], jnp.zeros((), jnp.bfloat16))
    expanded = expanded.reshape(height, adapter_table * device_rank)
    request_block = jnp.dot(part_attended, output_weight, preferred_element_type=jnp.float32)
    request_block = request_block + jnp.dot(
        expanded, flattened_up, preferred_element_type=jnp.float32
    )
    mixed = lax.psum_scatter(request_block, "tensor", scatter_dimension=0, tiled=True).astype(
        jnp.bfloat16
    )
    return (mixed, moved_cache)


def solution(mesh):
    peers, blocks = mesh.shape["dp"], mesh.shape["tensor"]
    body = functools.partial(fused_shards, peers, blocks) if peers == blocks == CACHE_STEP + 1 else shards
    in_specs = (
        P(("grp", "dp"), "tensor"),
        P(("grp", "dp"), None, None, "tensor"),
        P(("grp", "dp")),
        P(("grp", "dp")),
        P("dp", None, "tensor"),
        P(None, None, "dp"),
        P("tensor", "dp"),
    )
    out_specs = (P(("grp", "tensor"), "dp"), P(("grp", "dp"), None, None, "tensor"))
    return jax.shard_map(body, mesh=mesh, in_specs=in_specs, out_specs=out_specs, check_vma=False)
```

```python
import functools
import math

import jax
import jax.numpy as jnp
from jax import lax
from jax.experimental import pallas as pl
from jax.experimental.pallas import tpu as pltpu
from jax.sharding import PartitionSpec as P

HD = 128
LANES = 128
CACHE_STEP = 3
MESH = pl.DeviceIdType.MESH
F32 = jnp.float32
BF16 = jnp.bfloat16


def nt_dot(a, b):
    return lax.dot_general(a, b, (((1,), (1,)), ((), ())), preferred_element_type=F32)


def dot(a, b):
    return jnp.dot(a, b, preferred_element_type=F32)


def iota(shape, axis):
    return lax.broadcasted_iota(jnp.int32, shape, axis)


def flag(cond):
    return jnp.where(cond, 1.0, 0.0).astype(BF16)


def fused_kernel(
    peers,
    blocks,
    width,
    q_ref,
    cache_ref,
    len_ref,
    id_ref,
    down_hbm,
    up_hbm,
    w_hbm,
    mixed_ref,
    moved_ref,
    w_buf,
    up_buf,
    down_buf,
    att_buf,
    spread_buf,
    low_buf,
    low_in,
    own_buf,
    part_buf,
    part_recv,
    load_sem,
    att_send,
    att_recv,
    cache_send,
    cache_recv,
    low_send,
    low_recv,
    part_send_sem,
    part_recv_sem,
):
    dp = lax.axis_index("dp")
    tp = lax.axis_index("tensor")
    count, feats = q_ref.shape
    capacity = spread_buf.shape[1]
    out_width = w_buf.shape[1]
    chunk = part_buf.shape[3]
    chunks = out_width // chunk
    kv_heads = width // HD
    group = feats // width
    positions = cache_ref.shape[1] // (2 * width)

    loads = [
        pltpu.make_async_copy(down_hbm, down_buf, load_sem.at[0]),
        pltpu.make_async_copy(w_hbm, w_buf, load_sem.at[1]),
        pltpu.make_async_copy(up_hbm, up_buf, load_sem.at[2]),
    ]
    for load in loads:
        load.start()

    barrier = pltpu.get_barrier_semaphore()
    for d in range(peers):
        for e in range(blocks):
            if d or e:
                pl.semaphore_signal(
                    barrier,
                    inc=1,
                    device_id={"dp": lax.rem(dp + d, peers), "tensor": lax.rem(tp + e, blocks)},
                    device_id_type=MESH,
                )

    rows, cols = group * count, positions * count
    row_request = iota((rows, cols), 0) & (count - 1)
    col_index = iota((rows, cols), 1)
    col_request = col_index & (count - 1)
    tile_requests = flag(
        iota((count, cols), 0) == (iota((count, cols), 1) & (count - 1))
    )
    lengths = jnp.broadcast_to(len_ref[...], (16, count)).astype(F32).astype(BF16)
    limit = dot(lengths, tile_requests)[0:1, :] * float(count)
    live = (row_request == col_request) & (col_index.astype(F32) < limit)
    for g in range(kv_heads):
        query = jnp.concatenate(
            [q_ref[:, (g * group + h) * HD : (g * group + h + 1) * HD] for h in range(group)], 0
        )
        keys = jnp.concatenate(
            [
                cache_ref[:, 2 * j * width + g * HD : 2 * j * width + (g + 1) * HD]
                for j in range(positions)
            ],
            0,
        )
        values = jnp.concatenate(
            [
                cache_ref[:, (2 * j + 1) * width + g * HD : (2 * j + 1) * width + (g + 1) * HD]
                for j in range(positions)
            ],
            0,
        )
        scores = jnp.where(live, nt_dot(query, keys) * (1.0 / math.sqrt(HD)), -1e30)
        powers = jnp.exp(scores - jnp.max(scores, axis=1, keepdims=True))
        weights = (powers / jnp.sum(powers, axis=1, keepdims=True)).astype(BF16)
        output = dot(weights, values).astype(BF16)
        for h in range(group):
            att_buf[dp, :, (g * group + h) * HD : (g * group + h + 1) * HD] = output[
                h * count : (h + 1) * count
            ]

    ids = jnp.broadcast_to(id_ref[...], (LANES, count))
    chosen = iota((LANES, count), 0) == ids
    chosen_flag = flag(chosen)
    eye = flag(iota((count, count), 0) == iota((count, count), 1))
    att_buf[dp, :, feats : feats + LANES] = nt_dot(eye, chosen_flag).astype(BF16)

    pl.semaphore_wait(barrier, peers * blocks - 1)

    def att_copy(source, way):
        return pltpu.make_async_remote_copy(
            src_ref=att_buf.at[source],
            dst_ref=att_buf.at[source],
            send_sem=att_send.at[source, way],
            recv_sem=att_recv.at[source],
            device_id={"dp": lax.rem(dp + (1 if way else peers - 1), peers)},
            device_id_type=MESH,
        )

    def pass_on(source, act):
        @pl.when((source <= dp) & (dp < peers - 1))
        def _():
            act(att_copy(source, 1))

        @pl.when((source >= dp) & (dp > 0))
        def _():
            act(att_copy(source, 0))

    others = [lax.rem(dp + d, peers) for d in sorted(range(1, peers), key=lambda d: -min(d, peers - d))]
    pass_on(dp, lambda copy: copy.start())

    earlier = flag(iota((count, count), 0) < iota((count, count), 1))
    before = dot(chosen_flag, earlier)
    rank = jnp.sum(jnp.where(chosen, before, 0.0), axis=0, keepdims=True)
    place = id_ref[...].astype(F32) * float(capacity) + rank
    slots = peers * capacity
    move = flag(iota((slots, count), 0).astype(F32) == place)
    step = 512
    for c in range(cache_ref.shape[1] // step):
        piece = dot(move, cache_ref[:, c * step : (c + 1) * step]).astype(BF16)
        spread_buf[:, :, c * step : (c + 1) * step] = piece.reshape(peers, capacity, step)

    def cache_copy(target, source):
        return pltpu.make_async_remote_copy(
            src_ref=spread_buf.at[target],
            dst_ref=moved_ref.at[source],
            send_sem=cache_send.at[target],
            recv_sem=cache_recv.at[source],
            device_id={"dp": target},
            device_id_type=MESH,
        )

    own = pltpu.make_async_copy(spread_buf.at[dp], moved_ref.at[dp], load_sem.at[3])
    own.start()

    def low_copy(block, target, holder, part):
        return pltpu.make_async_remote_copy(
            src_ref=low_buf.at[block],
            dst_ref=low_in.at[holder, part],
            send_sem=low_send.at[block, target],
            recv_sem=low_recv.at[holder, part],
            device_id={"dp": target, "tensor": block},
            device_id_type=MESH,
        )

    def part_copy(block, part, c):
        return pltpu.make_async_remote_copy(
            src_ref=part_buf.at[block, c],
            dst_ref=part_recv.at[part, c],
            send_sem=part_send_sem.at[block, c],
            recv_sem=part_recv_sem.at[part, c],
            device_id={"tensor": block},
            device_id_type=MESH,
        )

    low_rank = down_buf.shape[1]
    held = flag(iota((LANES, low_rank), 0) == dp)
    loads[0].wait()
    loads[1].wait()

    def nearest(step):
        up = jnp.where(step - 1 < dp, step - 1, step)
        last = peers - step
        down = jnp.where(last > dp, last, last - 1)
        return jnp.where(step == 0, dp, jnp.where(dp < peers // 2, up, down))

    def arrive(step):
        source = nearest(step)
        att_copy(source, 0).wait_recv()
        pass_on(source, lambda copy: copy.start())

    inward = jnp.where(dp < peers // 2, lax.rem(dp + 1, peers), jnp.maximum(dp - 1, 0))
    inner = (dp > 0) & (dp < peers - 1)

    def work(step, carry):
        source = nearest(step)

        @pl.when((step > 0) & jnp.logical_not(inner & (step == 2)))
        def _():
            arrive(step)

        @pl.when((step == 1) & inner)
        def _():
            arrive(2)

        @pl.when(step == CACHE_STEP - 1)
        def _():
            cache_copy(inward, dp).start()

        @pl.when(step == CACHE_STEP)
        def _():
            for target in others:

                @pl.when(target != inward)
                def _():
                    cache_copy(target, dp).start()

        rows = att_buf[source, :, :feats]
        member = dot(att_buf[source, :, feats : feats + LANES], held)
        low_buf[source] = (nt_dot(rows, down_buf[0]) * member).astype(BF16)
        for target in others:
            low_copy(source, target, dp, tp).start()

        @pl.when(source != tp)
        def _():
            low_copy(source, dp, dp, tp).start()

        @pl.when(source == tp)
        def _():
            low_in[dp, tp] = low_buf[source]

        for c in range(chunks):
            at = slice(c * chunk, (c + 1) * chunk)
            part = dot(rows, w_buf[:, at])
            part_buf[source, c] = part.astype(BF16)

            @pl.when(source == tp)
            def _():
                own_buf[:, at] = part

            @pl.when(source != tp)
            def _():
                part_copy(source, tp, c).start()

        return carry

    lax.fori_loop(0, peers, work, 0)

    loads[2].wait()
    for d in range(peers):
        for e in range(blocks):
            if d or e:
                low_copy(tp, dp, lax.rem(dp + d, peers), lax.rem(tp + e, blocks)).wait_recv()
    lows = []
    for a in range(peers):
        total = low_in[a, 0].astype(F32)
        for t in range(1, blocks):
            total = total + low_in[a, t].astype(F32)
        lows.append(total)
    low_total = jnp.concatenate(lows, axis=1)
    high = low_total.astype(BF16)
    rest = (low_total - high.astype(F32)).astype(BF16)
    both = jnp.concatenate([high, rest], axis=0)
    for c in range(chunks):
        at = slice(c * chunk, (c + 1) * chunk)
        delta = dot(both, up_buf[:, :, at].reshape(peers * low_rank, chunk))
        own_buf[:, at] += delta[:count] + delta[count:]
    parts = [lax.rem(tp + e, blocks) for e in range(1, blocks)]
    for c in range(chunks):
        at = slice(c * chunk, (c + 1) * chunk)
        total = own_buf[:, at]
        for part in parts:
            part_copy(tp, part, c).wait_recv()
            total = total + part_recv[part, c].astype(F32)
        mixed_ref[:, at] = total.astype(BF16)

    own.wait()
    for source in others:
        cache_copy(dp, source).wait_recv()
    for target in others:
        cache_copy(target, dp).wait_send()
    for block in parts:
        for c in range(chunks):
            part_copy(block, tp, c).wait_send()
        low_copy(block, dp, dp, tp).wait_send()
    for block in range(blocks):
        pass_on(block, lambda copy: copy.wait_send())
        for target in others:
            low_copy(block, target, dp, tp).wait_send()


def fused_shards(
    peers,
    blocks,
    queries,
    key_value_cache,
    key_value_lengths,
    adapter_index,
    adapter_down_weight,
    adapter_up_weight,
    output_weight,
):
    count, feats = queries.shape
    capacity = max(2, 2 * count // peers)
    row = math.prod(key_value_cache.shape[1:])
    out_width = output_weight.shape[1]
    low_rank = adapter_down_weight.shape[1]
    height = peers * count
    chunks = 2
    vmem = pl.BlockSpec(memory_space=pltpu.VMEM)
    hbm = pl.BlockSpec(memory_space=pl.ANY)
    dma = pltpu.SemaphoreType.DMA
    mixed, moved = pl.pallas_call(
        functools.partial(fused_kernel, peers, blocks, key_value_cache.shape[-1]),
        out_shape=(
            jax.ShapeDtypeStruct((height // blocks, out_width), BF16),
            jax.ShapeDtypeStruct((peers, capacity, row), BF16),
        ),
        in_specs=[vmem, vmem, vmem, vmem, hbm, hbm, hbm],
        out_specs=(vmem, hbm),
        scratch_shapes=[
            pltpu.VMEM(output_weight.shape, BF16),
            pltpu.VMEM(adapter_up_weight.shape, BF16),
            pltpu.VMEM(adapter_down_weight.shape, BF16),
            pltpu.VMEM((peers, count, feats + LANES), BF16),
            pltpu.VMEM((peers, capacity, row), BF16),
            pltpu.VMEM((blocks, count, low_rank), BF16),
            pltpu.VMEM((peers, blocks, count, low_rank), BF16),
            pltpu.VMEM((count, out_width), F32),
            pltpu.VMEM((blocks, chunks, count, out_width // chunks), BF16),
            pltpu.VMEM((blocks, chunks, count, out_width // chunks), BF16),
            dma((4,)),
            dma((peers, 2)),
            dma((peers,)),
            dma((peers,)),
            dma((peers,)),
            dma((blocks, peers)),
            dma((peers, blocks)),
            dma((blocks, chunks)),
            dma((blocks, chunks)),
        ],
        compiler_params=pltpu.CompilerParams(
            collective_id=0, has_side_effects=True, vmem_limit_bytes=56 * 1024 * 1024
        ),
        name="fused",
    )(
        queries,
        key_value_cache.reshape(count, row),
        key_value_lengths.reshape(1, count),
        adapter_index.reshape(1, count),
        adapter_down_weight,
        adapter_up_weight,
        output_weight,
    )
    return mixed, moved.reshape((peers * capacity,) + key_value_cache.shape[1:])


def earlier_same(targets):
    count = targets.shape[0]
    order = jnp.arange(count, dtype=jnp.int32)
    same = targets[:, None] == targets[None, :]
    before = order[None, :] < order[:, None]
    return jnp.sum(jnp.where(same & before, 1, 0), axis=1).astype(jnp.int32)


def attend(queries, cache, lengths):
    count = queries.shape[0]
    width = cache.shape[-1]
    kv_heads = width // HD
    group = queries.shape[1] // width
    query = queries.reshape(count, kv_heads, group, HD)
    keys = cache[:, :, 0, :].reshape(count, -1, kv_heads, HD)
    values = cache[:, :, 1, :].reshape(count, -1, kv_heads, HD)
    scores = jnp.einsum("rhgd,rlhd->rhgl", query, keys, preferred_element_type=jnp.float32) * (
        1.0 / math.sqrt(HD)
    )
    position = jnp.arange(keys.shape[1], dtype=jnp.int32)
    live = position[None, None, None, :] < lengths[:, None, None, None]
    scores = jnp.where(live, scores, -1e30)
    highest = jnp.max(scores, axis=-1, keepdims=True)
    powers = jnp.exp(scores - highest)
    weights = (powers / jnp.sum(powers, axis=-1, keepdims=True)).astype(jnp.bfloat16)
    output = jnp.einsum("rhgl,rlhd->rhgd", weights, values, preferred_element_type=jnp.float32)
    return output.reshape(count, -1).astype(jnp.bfloat16)


def down_projection(attended_rows, adapter_down_weight):
    product = lax.dot_general(
        attended_rows,
        adapter_down_weight[0],
        (((1,), (1,)), ((), ())),
        preferred_element_type=jnp.float32,
    )
    return product.astype(jnp.bfloat16)


def shards(
    queries,
    key_value_cache,
    key_value_lengths,
    adapter_index,
    adapter_down_weight,
    adapter_up_weight,
    output_weight,
):
    peers = lax.axis_size("dp")
    count = queries.shape[0]
    capacity = max(2, 2 * count // peers)
    slots = peers * capacity
    places = adapter_index * capacity + earlier_same(adapter_index)

    def spread(values):
        return jnp.zeros((slots,) + values.shape[1:], values.dtype).at[places].set(values)

    attended_rows = attend(queries, key_value_cache, key_value_lengths)
    moved_attended, moved_cache = (
        lax.all_to_all(spread(attended_rows), "dp", split_axis=0, concat_axis=0, tiled=True),
        lax.all_to_all(spread(key_value_cache), "dp", split_axis=0, concat_axis=0, tiled=True),
    )
    low_rank_output = down_projection(moved_attended, adapter_down_weight)
    lowered = lax.all_to_all(low_rank_output, "dp", split_axis=0, concat_axis=0, tiled=True)[places]
    adapter_table = adapter_up_weight.shape[0]
    device_rank = adapter_up_weight.shape[1]
    flattened_up = adapter_up_weight.reshape(
        adapter_table * device_rank, adapter_up_weight.shape[2]
    )
    part_attended = lax.all_gather(attended_rows, "dp", axis=0, tiled=True)
    part_lowered = lax.all_gather(lowered, "dp", axis=0, tiled=True)
    part_ids = lax.all_gather(adapter_index, "dp", axis=0, tiled=True)
    height = part_attended.shape[0]
    chosen = part_ids[:, None] == jnp.arange(adapter_table, dtype=jnp.int32)[None, :]
    expanded = jnp.where(chosen[:, :, None], part_lowered[:, None, :], jnp.zeros((), jnp.bfloat16))
    expanded = expanded.reshape(height, adapter_table * device_rank)
    request_block = jnp.dot(part_attended, output_weight, preferred_element_type=jnp.float32)
    request_block = request_block + jnp.dot(
        expanded, flattened_up, preferred_element_type=jnp.float32
    )
    mixed = lax.psum_scatter(request_block, "tensor", scatter_dimension=0, tiled=True).astype(
        jnp.bfloat16
    )
    return (mixed, moved_cache)


def solution(mesh):
    peers, blocks = mesh.shape["dp"], mesh.shape["tensor"]
    body = functools.partial(fused_shards, peers, blocks) if peers == blocks == CACHE_STEP + 1 else shards
    in_specs = (
        P(("grp", "dp"), "tensor"),
        P(("grp", "dp"), None, None, "tensor"),
        P(("grp", "dp")),
        P(("grp", "dp")),
        P("dp", None, "tensor"),
        P(None, None, "dp"),
        P("tensor", "dp"),
    )
    out_specs = (P(("grp", "tensor"), "dp"), P(("grp", "dp"), None, None, "tensor"))
    return jax.shard_map(body, mesh=mesh, in_specs=in_specs, out_specs=out_specs, check_vma=False)
```
